256 devices in a mesh: gx: 16 (over z_lo, y, core), gy: 16 (over x, z_hi).
Axes of the slice: x: 4, y: 4, z: 8 (z_hi: 4, z_lo: 2; z = z_hi * 2 + z_lo), core: 2. Of those that a mesh axis runs over, the one named last changes fastest.
Arguments:
- tokens: bfloat16 [1536, 6144], P('gy', 'gx'), may hold values from -6 to 6
- weight_in: bfloat16 [6144, 24576], P('gx', 'gy'), may hold values from -0.078125 to 0.078125
- tangent_in: bfloat16 [6144, 24576], P('gx', 'gy'), may hold values from -0.078125 to 0.078125
- weight_out: bfloat16 [24576, 6144], P('gy', 'gx'), may hold values from -0.0390625 to 0.0390625
- tangent_out: bfloat16 [24576, 6144], P('gy', 'gx'), may hold values from -0.0390625 to 0.0390625
- curvature: float32 [1536, 6144], P(None, 'gx'), may hold values from 0.2 to 4
Outputs:
- grad_in: float32 [6144, 24576], P('gx', 'gy')
- grad_out: float32 [24576, 6144], P('gy', 'gx')
The draws below stay inside these ranges and needn't reach their ends.
All inputs are finite; a program needn't handle non-finite values.
Results may differ from the reference program's by a relative error of at most 0.0059.
Values may be sent and summed in bfloat16 or wider, within the bound.
No kernel may reach another device: no remote copies, remote signals or barrier semaphores. Data moves between devices by JAX's collectives and lax.ppermute only.
A program may use at most 128 MiB of HBM per device.

```python
import math
import jax
import jax.numpy as jnp
from jax import lax

D = 6144
FF = 24576
TOKENS = 1536


def shard_levels(own_key, extent, cuts, least, top_value):
    def one(axis_at, shards_of):
        heights = jax.random.uniform(jax.random.fold_in(jax.random.fold_in(own_key, 6), axis_at), (shards_of,), jnp.float32, least / len(cuts), top_value / len(cuts))
        return jnp.repeat(jnp.exp(heights), extent[axis_at] // shards_of).reshape((-1,) + (1,) * (len(extent) - axis_at - 1))

    factor_of = one(*cuts[0])
    for cut in cuts[1:]:
        factor_of = factor_of * one(*cut)
    return factor_of


def centred(own_key, extent, width, reach, pieces=(), held_as=jnp.bfloat16):
    drawn = width * jax.random.normal(own_key, extent, jnp.float32)
    if pieces:
        drawn = drawn * shard_levels(own_key, extent, pieces, -0.22, 0.18)
    return jnp.clip(drawn, -reach, reach).astype(held_as)


def setup_inputs(seed: int = 0) -> dict:
    streams_of = jax.random.split(jax.random.key(seed), 7)
    tokens = centred(streams_of[0], (TOKENS, D), 1.0, 6.0, ((0, 16), (1, 16)))
    weight_in = centred(streams_of[1], (D, FF), D ** -0.5, 0.078125, ((0, 16), (1, 16)))
    tangent_in = centred(streams_of[2], (D, FF), D ** -0.5, 0.078125, ((0, 16), (1, 16)))
    weight_out = centred(streams_of[3], (FF, D), FF ** -0.5, 0.0390625, ((0, 16), (1, 16)))
    tangent_out = centred(streams_of[4], (FF, D), FF ** -0.5, 0.0390625, ((0, 16), (1, 16)))
    curvature = jnp.clip(jnp.exp(math.log(4.0) - 2.9957323 * jax.random.uniform(streams_of[5], (TOKENS, D), jnp.float32) ** shard_levels(streams_of[5], (TOKENS, D), ((1, 16),), -0.2, 0.2)), 0.2, 4.0)
    return {"tokens": tokens, "weight_in": weight_in, "tangent_in": tangent_in, "weight_out": weight_out, "tangent_out": tangent_out, "curvature": curvature}


def gelu_value(pre_act):
    return 0.5 * pre_act * (1.0 + jax.scipy.special.erf(pre_act / math.sqrt(2.0)))

def gelu_slope(pre_act):
    cdf_part = 0.5 * (1.0 + jax.scipy.special.erf(pre_act / math.sqrt(2.0)))
    return cdf_part + pre_act * jnp.exp(-0.5 * pre_act * pre_act) / math.sqrt(2.0 * math.pi)

def reference(tokens, weight_in, tangent_in, weight_out, tangent_out, curvature):
    pre_act = jnp.dot(tokens, weight_in, preferred_element_type=jnp.float32)
    pre_tan = jnp.dot(tokens, tangent_in, preferred_element_type=jnp.float32)
    slopes = gelu_slope(pre_act)
    acts = gelu_value(pre_act).astype(jnp.bfloat16)
    dacts = (slopes * pre_tan).astype(jnp.bfloat16)
    out_tan = jnp.dot(dacts, weight_out, preferred_element_type=jnp.float32) + jnp.dot(acts, tangent_out, preferred_element_type=jnp.float32)
    weighted = (curvature * out_tan).astype(jnp.bfloat16)
    back_act = lax.dot_general(weighted, weight_out, (((1,), (1,)), ((), ())), preferred_element_type=jnp.float32)
    back_pre = (slopes * back_act).astype(jnp.bfloat16)
    scale = 1.0 / math.sqrt(TOKENS)
    grad_in = lax.dot_general(tokens, back_pre, (((0,), (0,)), ((), ())), preferred_element_type=jnp.float32) * scale
    grad_out = lax.dot_general(acts, weighted, (((0,), (0,)), ((), ())), preferred_element_type=jnp.float32) * scale
    return (grad_in, grad_out)
```

```python
import math

import jax
import jax.numpy as jnp
from jax import lax
from jax.sharding import Mesh
from jax.sharding import PartitionSpec as P

BF16 = jnp.bfloat16
F32 = jnp.float32
RING = 4


def gelu_parts(pre_act):
    cdf = 0.5 * (1.0 + lax.erf(pre_act / math.sqrt(2.0)))
    slopes = cdf + pre_act * jnp.exp(-0.5 * pre_act * pre_act) / math.sqrt(2.0 * math.pi)
    return pre_act * cdf, slopes


def shift(value, axis, by):
    return lax.ppermute(value, axis, [(i, (i + by) % RING) for i in range(RING)])


def swap(value, axis):
    return lax.ppermute(value, axis, [(0, 1), (1, 0)])


def part(value, dim, start, size=1):
    return lax.slice_in_dim(value, start, start + size, axis=dim)


def halves(value, dim):
    size = value.shape[dim] // 2
    return part(value, dim, 0, size), part(value, dim, size, size)


def join(parts, dim):
    return lax.concatenate(parts, dim)


def ring_sum(block, axis):
    got = [shift(block(k).astype(BF16), axis, k) for k in (2, 1, 3)]
    total = block(0).astype(F32)
    for value in got:
        total = total + value.astype(F32)
    return total


def ring_gather(own, axis):
    got = {k: shift(own, axis, -k) for k in (2, 1, 3)}
    return [own, got[1], got[2], got[3]]


def pick(value, dim, index):
    return lax.dynamic_slice_in_dim(value, index, 1, axis=dim)


def rolled(blocks, dim, offset):
    return lax.dynamic_slice_in_dim(join(blocks + blocks[:-1], dim), offset, RING, axis=dim)


def pair_sum(value, axis, dim):
    own, other = halves(value, dim)
    return own.astype(F32) + swap(other.astype(BF16), axis).astype(F32)


def gx_sum(block4, kind):
    if kind == "wide":
        return pair_sum(ring_sum(lambda k: part(block4, 0, k), "y"), "zl", 1)
    first = pair_sum(block4, "zl", 0)
    return ring_sum(lambda k: part(first, 1, k), "y")


def gx_gather(own, kind):
    if kind == "wide":
        both = join([own, swap(own, "zl")], 1)
        return join(ring_gather(both, "y"), 0)
    four = join(ring_gather(own, "y"), 1)
    return join([four, swap(four, "zl")], 0)


def gy_sum(block4, ox, oz):
    first = ring_sum(
        lambda k: join([pick(b, 0, (k - i) % RING) for b, i in zip(block4, ox)], 2), "x"
    )
    groups = [part(first, 2, g * (first.shape[2] // len(ox)), first.shape[2] // len(ox)) for g in range(len(ox))]
    return ring_sum(lambda k: join([pick(b, 1, (k - i) % RING) for b, i in zip(groups, oz)], 2), "zh")


def gy_gather(own, ox, oz):
    blocks = ring_gather(own, "zh")
    size = own.shape[2] // len(ox)

    def of_group(values, g):
        return [part(v, 2, g * size, size) for v in values]

    column = join([rolled(of_group(blocks, g), 1, i) for g, i in enumerate(oz)], 2)
    blocks = ring_gather(column, "x")
    return [rolled(of_group(blocks, g), 0, i) for g, i in enumerate(ox)]


def dot(a, b, contract):
    return lax.dot_general(a, b, ((contract[:1], contract[1:]), ((), ())), preferred_element_type=F32)


def per_device(tokens, weight_in, tangent_in, weight_out, tangent_out, curvature):
    core, y, zl = lax.axis_index("c"), lax.axis_index("y"), lax.axis_index("zl")
    gy = lax.axis_index("x") * RING + lax.axis_index("zh")
    rows, width = tokens.shape
    hidden = weight_in.shape[1]
    half = rows // 2
    quarter = half // 2
    scale = 1.0 / math.sqrt(rows * 16)

    keep = lax.dynamic_slice_in_dim(tokens, core * half, half, 0)
    give = lax.dynamic_slice_in_dim(tokens, (1 - core) * half, half, 0)
    own_rows = join([keep, swap(give, "c")], 1)
    curv = lax.dynamic_slice_in_dim(curvature, gy * rows, rows, 0)
    curv_keep = lax.dynamic_slice_in_dim(curv, core * half, half, 0)
    curv_give = lax.dynamic_slice_in_dim(curv, (1 - core) * half, half, 0)

    kinds = ("wide", "deep")
    offsets = {"wide": (y, 2 * zl), "deep": (2 * zl, y)}
    mine = own_rows.reshape(1, 1, half, 2 * width)
    every_ox, every_oz = zip(*(offsets[kind] for kind in kinds))
    toks = {
        kind: value.reshape(-1, 2 * width)
        for kind, value in zip(kinds, gy_gather(mine, every_ox, every_oz))
    }
    w_in = join([weight_in, swap(weight_in, "c")], 0)
    t_in = join([tangent_in, swap(tangent_in, "c")], 0)
    curv_own = join([curv_keep, swap(curv_give, "c")], 1)
    w_out_other = swap(weight_out, "c")
    out_side = join(
        [
            join([tangent_out, swap(tangent_out, "c")], 1),
            join([weight_out, w_out_other], 1),
        ],
        0,
    )
    w_out = part(out_side, 0, hidden, hidden)

    def group(value):
        return value.reshape(RING, RING, quarter, -1)

    slopes, hidden_all, weighted_all, back_all = {}, {}, {}, {}
    for kind in kinds:
        both = join(
            [dot(toks[kind], w_in, (1, 0)), dot(toks[kind], t_in, (1, 0))], 1
        )
        both = gx_sum(group(both), kind)
        pre_act, pre_tan = halves(both, 3)
        acts, slopes[kind] = gelu_parts(pre_act)
        dacts = slopes[kind] * pre_tan
        hidden_all[kind] = gx_gather(join([acts.astype(BF16), dacts.astype(BF16)], 3), kind).reshape(
            -1, 2 * hidden
        )
    out_parts = [group(dot(hidden_all[kind], out_side, (1, 0))) for kind in kinds]
    out_tan = gy_sum(out_parts, every_ox, every_oz)
    weighted = (curv_own.reshape(out_tan.shape) * out_tan).astype(BF16)
    weighted_all = {
        kind: value.reshape(-1, 2 * width)
        for kind, value in zip(kinds, gy_gather(weighted, every_ox, every_oz))
    }
    for kind in kinds:
        back = dot(weighted_all[kind], w_out, (1, 1))
        back = gx_sum(group(back), kind)
        back_all[kind] = gx_gather((slopes[kind] * back).astype(BF16), kind).reshape(-1, hidden)

    every = {
        name: join([table[kind] for kind in kinds], 0)
        for name, table in (("t", toks), ("h", hidden_all), ("w", weighted_all), ("b", back_all))
    }
    acts_all = part(every["h"], 1, 0, hidden)
    w_mine, w_theirs = halves(every["w"], 1)
    t_mine, t_theirs = halves(every["t"], 1)
    out_got = swap(dot(acts_all, w_theirs, (0, 0)), "c")
    grad_out = (dot(acts_all, w_mine, (0, 0)) + out_got.astype(F32)) * scale
    in_got = swap(dot(t_theirs, every["b"], (0, 0)), "c")
    grad_in = (dot(t_mine, every["b"], (0, 0)) + in_got.astype(F32)) * scale
    return grad_in, grad_out


def solution(mesh):
    fine = Mesh(mesh.devices.reshape(2, 4, 2, 4, 4), ("zl", "y", "c", "x", "zh"))
    gx, gy = ("zl", "y", "c"), ("x", "zh")
    return jax.shard_map(
        per_device,
        mesh=fine,
        in_specs=(P(gy, gx), P(gx, gy), P(gx, gy), P(gy, gx), P(gy, gx), P(None, gx)),
        out_specs=(P(gx, gy), P(gy, gx)),
        check_vma=False,
    )
```

```python
import math

import jax
import jax.numpy as jnp
from jax import lax
from jax.sharding import Mesh
from jax.sharding import PartitionSpec as P

BF16 = jnp.bfloat16
F32 = jnp.float32
RING = 4


def gelu_parts(pre_act):
    cdf = 0.5 * (1.0 + lax.erf(pre_act / math.sqrt(2.0)))
    slopes = cdf + pre_act * jnp.exp(-0.5 * pre_act * pre_act) / math.sqrt(2.0 * math.pi)
    return pre_act * cdf, slopes


def shift(value, axis, by):
    return lax.ppermute(value, axis, [(i, (i + by) % RING) for i in range(RING)])


def swap(value, axis):
    return lax.ppermute(value, axis, [(0, 1), (1, 0)])


def part(value, dim, start, size=1):
    return lax.slice_in_dim(value, start, start + size, axis=dim)


def halves(value, dim):
    size = value.shape[dim] // 2
    return part(value, dim, 0, size), part(value, dim, size, size)


def join(parts, dim):
    return lax.concatenate(parts, dim)


def ring_send(block, axis):
    return [shift(block(k).astype(BF16), axis, k) for k in (1, 3, 2)]


def total(own, got):
    own = own.astype(F32)
    for value in got:
        own = own + value.astype(F32)
    return own


def ring_sum(block, axis):
    return total(block(0), ring_send(block, axis))


def ring_gather(own, axis):
    got = lax.optimization_barrier([shift(own, axis, -k) for k in (1, 3, 2)])
    return [own, got[0], got[2], got[1]]


def pick(value, dim, index, size=1):
    return lax.dynamic_slice_in_dim(value, index, size, axis=dim)


def rolled(value, dim, offset):
    twice = join([value, part(value, dim, 0, RING - 1)], dim)
    return lax.dynamic_slice_in_dim(twice, offset, RING, axis=dim)


def gx_sum(wide, deep, y, zl, work, aside):
    def zl_half(value, dim):
        return lambda m: pick(value, dim, 2 * ((zl + m) % 2), 2)

    wide_block, deep_block = lambda k: pick(wide, 0, (y + k) % RING), zl_half(deep, 0)
    wide_own, deep_own, wide_out, deep_out, aside = lax.optimization_barrier(
        (
            wide_block(0).astype(F32),
            deep_block(0).astype(F32),
            {k: wide_block(k).astype(BF16) for k in range(1, RING)},
            deep_block(1).astype(BF16),
            aside,
        )
    )
    deep_got = swap(deep_out, "zl")
    wide_got, deep_got, done = lax.optimization_barrier(
        (ring_send(lambda k: wide_out[k], "y"), deep_got, work(aside))
    )
    wide = total(wide_own, wide_got)
    deep = total(deep_own, [deep_got])

    wide_block, deep_block = zl_half(wide, 1), lambda k: pick(deep, 1, (y + k) % RING)
    wide_got = swap(wide_block(1).astype(BF16), "zl")
    deep_got, wide_got = lax.optimization_barrier((ring_send(deep_block, "y"), wide_got))
    return (total(wide_block(0), [wide_got]), total(deep_block(0), deep_got)), done


def gx_gather(wide, deep):
    deep_got, wide_got = lax.optimization_barrier((ring_gather(deep, "y"), swap(wide, "zl")))
    wide = join([wide, wide_got], 1)
    deep = join(deep_got, 1)
    wide_got, deep_got = lax.optimization_barrier((ring_gather(wide, "y"), swap(deep, "zl")))
    return join(wide_got, 0), join([deep, deep_got], 0)


def gy_sum(block4s, offsets):
    count = len(block4s)
    first = ring_sum(
        lambda k: join([pick(b, 0, (k - ox) % RING) for b, (ox, _) in zip(block4s, offsets)], 2), "x"
    )
    size = first.shape[2] // count
    columns = [part(first, 2, g * size, size) for g in range(count)]
    return ring_sum(
        lambda k: join([pick(c, 1, (k - oz) % RING) for c, (_, oz) in zip(columns, offsets)], 2), "zh"
    )


def split_groups(blocks, groups):
    size = blocks[0].shape[2] // groups
    return [join([part(b, 2, g * size, size) for b in blocks], 0) for g in range(groups)]


def gy_gather(own, groups):
    return split_groups(ring_gather(join(ring_gather(own, "zh"), 1), "x"), groups)


def ring_order(block4, offset):
    ox, oz = offset
    return rolled(rolled(block4, 0, ox), 1, oz)


def dot(a, b, contract):
    return lax.dot_general(a, b, ((contract[:1], contract[1:]), ((), ())), preferred_element_type=F32)


def per_device(tokens, weight_in, tangent_in, weight_out, tangent_out, curvature):
    core, y, zl = lax.axis_index("c"), lax.axis_index("y"), lax.axis_index("zl")
    gy = lax.axis_index("x") * RING + lax.axis_index("zh")
    rows, width = tokens.shape
    hidden = weight_in.shape[1]
    half = rows // 2
    quarter = half // 2
    scale = 1.0 / math.sqrt(rows * 16)

    keep = lax.dynamic_slice_in_dim(tokens, core * half, half, 0)
    give = lax.dynamic_slice_in_dim(tokens, (1 - core) * half, half, 0)
    curv = lax.dynamic_slice_in_dim(curvature, gy * rows, rows, 0)
    curv_keep = lax.dynamic_slice_in_dim(curv, core * half, half, 0)
    curv_give = lax.dynamic_slice_in_dim(curv, (1 - core) * half, half, 0)

    kinds = ("wide", "deep")
    offsets = {"wide": (y, 2 * zl), "deep": (2 * zl, y)}
    places = [offsets[kind] for kind in kinds]
    got, curv_got = lax.optimization_barrier((swap(give, "c"), swap(curv_give, "c")))
    own_rows = join([keep, got], 1).reshape(1, 1, half, 2 * width)
    curv_own = join([curv_keep, curv_got], 1)
    w_got, t_got = swap(weight_in, "c"), swap(tangent_in, "c")
    column = join(ring_gather(own_rows, "zh"), 1)
    column, w_got, t_got, w_out_own, t_out_own = lax.optimization_barrier(
        (column, w_got, t_got, weight_out, tangent_out)
    )
    w_out_got, t_out_got = swap(w_out_own, "c"), swap(t_out_own, "c")
    blocks = ring_gather(column, "x")
    blocks, w_out_got, t_out_got = lax.optimization_barrier((blocks, w_out_got, t_out_got))
    toks = dict(zip(kinds, split_groups(blocks, len(kinds))))
    w_in = join([weight_in, w_got], 0)
    t_in = join([tangent_in, t_got], 0)
    out_side = join([join([tangent_out, t_out_got], 1), join([weight_out, w_out_got], 1)], 0)
    w_out = part(out_side, 0, hidden, hidden)

    def flat(value):
        return value.reshape(-1, value.shape[-1])

    def group(value):
        return value.reshape(RING, RING, quarter, -1)

    def all_in_ring_order(values):
        return join([flat(ring_order(values[kind], offsets[kind])) for kind in kinds], 0)

    pres = [
        group(join([dot(flat(toks[kind]), w_in, (1, 0)), dot(flat(toks[kind]), t_in, (1, 0))], 1))
        for kind in kinds
    ]
    slopes, mixed = [], []
    pre_sums, tokens_all = gx_sum(*pres, y, zl, all_in_ring_order, toks)
    for both in pre_sums:
        pre_act, pre_tan = halves(both, 3)
        acts, slope = gelu_parts(pre_act)
        slopes.append(slope)
        mixed.append(join([acts.astype(BF16), (slope * pre_tan).astype(BF16)], 3))
    hidden_all = dict(zip(kinds, gx_gather(*mixed)))
    out_tan = gy_sum([group(dot(flat(hidden_all[kind]), out_side, (1, 0))) for kind in kinds], places)
    weighted = (curv_own.reshape(out_tan.shape) * out_tan).astype(BF16)
    weighted_all = dict(zip(kinds, gy_gather(weighted, len(kinds))))
    back_parts = [group(dot(flat(weighted_all[kind]), w_out, (1, 1))) for kind in kinds]
    backs, weighted_all = gx_sum(*back_parts, y, zl, all_in_ring_order, weighted_all)
    back_pres = [(slope * back).astype(BF16) for slope, back in zip(slopes, backs)]
    back_all = dict(zip(kinds, gx_gather(*back_pres)))

    hidden_rows = join([flat(hidden_all[kind]) for kind in kinds], 0)
    back_rows = join([flat(back_all[kind]) for kind in kinds], 0)
    acts_all = part(hidden_rows, 1, 0, hidden)
    w_mine, w_theirs = halves(weighted_all, 1)
    t_mine, t_theirs = halves(tokens_all, 1)
    out_got = swap(dot(acts_all, w_theirs, (0, 0)), "c")
    grad_out = (dot(acts_all, w_mine, (0, 0)) + out_got.astype(F32)) * scale
    in_got = swap(dot(t_theirs, back_rows, (0, 0)), "c")
    grad_in = (dot(t_mine, back_rows, (0, 0)) + in_got.astype(F32)) * scale
    return grad_in, grad_out


def solution(mesh):
    fine = Mesh(mesh.devices.reshape(2, 4, 2, 4, 4), ("zl", "y", "c", "x", "zh"))
    gx, gy = ("zl", "y", "c"), ("x", "zh")
    return jax.shard_map(
        per_device,
        mesh=fine,
        in_specs=(P(gy, gx), P(gx, gy), P(gx, gy), P(gy, gx), P(gy, gx), P(None, gx)),
        out_specs=(P(gx, gy), P(gy, gx)),
        check_vma=False,
    )
```

```python
import math

import jax
import jax.numpy as jnp
from jax import lax
from jax.sharding import Mesh
from jax.sharding import PartitionSpec as P

BF16 = jnp.bfloat16
F32 = jnp.float32
RING = 4


def gelu_parts(pre_act):
    cdf = 0.5 * (1.0 + lax.erf(pre_act / math.sqrt(2.0)))
    slopes = cdf + pre_act * jnp.exp(-0.5 * pre_act * pre_act) / math.sqrt(2.0 * math.pi)
    return pre_act * cdf, slopes


def shift(value, axis, by):
    return lax.ppermute(value, axis, [(i, (i + by) % RING) for i in range(RING)])


def swap(value, axis):
    return lax.ppermute(value, axis, [(0, 1), (1, 0)])


def part(value, dim, start, size=1):
    return lax.slice_in_dim(value, start, start + size, axis=dim)


def halves(value, dim):
    size = value.shape[dim] // 2
    return part(value, dim, 0, size), part(value, dim, size, size)


def join(parts, dim):
    return lax.concatenate(parts, dim)


def ring_send(block, axis):
    return [shift(block(k).astype(BF16), axis, k) for k in (1, 3, 2)]


def total(own, got):
    own = own.astype(F32)
    for value in got:
        own = own + value.astype(F32)
    return own


def ring_sum(block, axis):
    return total(block(0), ring_send(block, axis))


def ring_gather(own, axis):
    got = lax.optimization_barrier([shift(own, axis, -k) for k in (1, 3, 2)])
    return [own, got[0], got[2], got[1]]


def pick(value, dim, index, size=1):
    return lax.dynamic_slice_in_dim(value, index, size, axis=dim)


def rolled(value, dim, offset):
    twice = join([value, part(value, dim, 0, RING - 1)], dim)
    return lax.dynamic_slice_in_dim(twice, offset, RING, axis=dim)


def gx_sum(wide, deep, y, zl, work, aside):
    def zl_half(value, dim):
        return lambda m: pick(value, dim, 2 * ((zl + m) % 2), 2)

    wide_block, deep_block = lambda k: pick(wide, 0, (y + k) % RING), zl_half(deep, 0)
    wide_own, deep_own, wide_out, deep_out, aside = lax.optimization_barrier(
        (
            wide_block(0).astype(F32),
            deep_block(0).astype(F32),
            {k: wide_block(k).astype(BF16) for k in range(1, RING)},
            deep_block(1).astype(BF16),
            aside,
        )
    )
    deep_got = swap(deep_out, "zl")
    wide_got, deep_got, done = lax.optimization_barrier(
        (ring_send(lambda k: wide_out[k], "y"), deep_got, work(aside))
    )
    wide = total(wide_own, wide_got)
    deep = total(deep_own, [deep_got])

    wide_block, deep_block = zl_half(wide, 1), lambda k: pick(deep, 1, (y + k) % RING)
    wide_got = swap(wide_block(1).astype(BF16), "zl")
    deep_got, wide_got = lax.optimization_barrier((ring_send(deep_block, "y"), wide_got))
    return (total(wide_block(0), [wide_got]), total(deep_block(0), deep_got)), done


def gx_gather(wide, deep):
    deep_got, wide_got = lax.optimization_barrier((ring_gather(deep, "y"), swap(wide, "zl")))
    wide = join([wide, wide_got], 1)
    deep = join(deep_got, 1)
    wide_got, deep_got = lax.optimization_barrier((ring_gather(wide, "y"), swap(deep, "zl")))
    return join(wide_got, 0), join([deep, deep_got], 0)


def gy_sum(block4s, offsets):
    count = len(block4s)
    first = ring_sum(
        lambda k: join([pick(b, 0, (k - ox) % RING) for b, (ox, _) in zip(block4s, offsets)], 2), "x"
    )
    size = first.shape[2] // count
    columns = [part(first, 2, g * size, size) for g in range(count)]
    return ring_sum(
        lambda k: join([pick(c, 1, (k - oz) % RING) for c, (_, oz) in zip(columns, offsets)], 2), "zh"
    )


def split_groups(blocks, groups):
    size = blocks[0].shape[2] // groups
    return [join([part(b, 2, g * size, size) for b in blocks], 0) for g in range(groups)]


def gy_gather(own, groups):
    return split_groups(ring_gather(join(ring_gather(own, "zh"), 1), "x"), groups)


def ring_order(block4, offset):
    ox, oz = offset
    return rolled(rolled(block4, 0, ox), 1, oz)


def dot(a, b, contract):
    return lax.dot_general(a, b, ((contract[:1], contract[1:]), ((), ())), preferred_element_type=F32)


def per_device(tokens, weight_in, tangent_in, weight_out, tangent_out, curvature):
    core, y, zl = lax.axis_index("c"), lax.axis_index("y"), lax.axis_index("zl")
    gy = lax.axis_index("x") * RING + lax.axis_index("zh")
    rows, width = tokens.shape
    hidden = weight_in.shape[1]
    half = rows // 2
    quarter = half // 2
    scale = 1.0 / math.sqrt(rows * 16)

    keep = lax.dynamic_slice_in_dim(tokens, core * half, half, 0)
    give = lax.dynamic_slice_in_dim(tokens, (1 - core) * half, half, 0)
    curv = lax.dynamic_slice_in_dim(curvature, gy * rows, rows, 0)
    curv_keep = lax.dynamic_slice_in_dim(curv, core * half, half, 0)
    curv_give = lax.dynamic_slice_in_dim(curv, (1 - core) * half, half, 0)

    kinds = ("wide", "deep")
    offsets = {"wide": (y, 2 * zl), "deep": (2 * zl, y)}
    places = [offsets[kind] for kind in kinds]
    got, curv_got = lax.optimization_barrier((swap(give, "c"), swap(curv_give, "c")))
    own_rows = join([keep, got], 1).reshape(1, 1, half, 2 * width)
    curv_own = join([curv_keep, curv_got], 1)
    w_got, t_got = swap(weight_in, "c"), swap(tangent_in, "c")
    column = join(ring_gather(own_rows, "zh"), 1)
    column, w_got, t_got, w_out_own, t_out_own = lax.optimization_barrier(
        (column, w_got, t_got, weight_out, tangent_out)
    )
    w_out_got, t_out_got = swap(w_out_own, "c"), swap(t_out_own, "c")
    blocks = ring_gather(column, "x")
    blocks, w_out_got, t_out_got = lax.optimization_barrier((blocks, w_out_got, t_out_got))
    toks = dict(zip(kinds, split_groups(blocks, len(kinds))))
    w_in = join([weight_in, w_got], 0)
    t_in = join([tangent_in, t_got], 0)
    out_side = join([join([tangent_out, t_out_got], 1), join([weight_out, w_out_got], 1)], 0)
    w_out = part(out_side, 0, hidden, hidden)

    def flat(value):
        return value.reshape(-1, value.shape[-1])

    def group(value):
        return value.reshape(RING, RING, quarter, -1)

    def all_in_ring_order(values):
        return join([flat(ring_order(values[kind], offsets[kind])) for kind in kinds], 0)

    pres = [
        group(join([dot(flat(toks[kind]), w_in, (1, 0)), dot(flat(toks[kind]), t_in, (1, 0))], 1))
        for kind in kinds
    ]
    slopes, mixed = [], []
    pre_sums, tokens_all = gx_sum(*pres, y, zl, all_in_ring_order, toks)
    for both in pre_sums:
        pre_act, pre_tan = halves(both, 3)
        acts, slope = gelu_parts(pre_act)
        slopes.append(slope)
        mixed.append(join([acts.astype(BF16), (slope * pre_tan).astype(BF16)], 3))
    hidden_rows = join([flat(value) for value in gx_gather(*mixed)], 0)
    out_parts = [group(value) for value in halves(dot(hidden_rows, out_side, (1, 0)), 0)]
    out_tan = gy_sum(out_parts, places)
    weighted = (curv_own.reshape(out_tan.shape) * out_tan).astype(BF16)
    weighted_all = dict(zip(kinds, gy_gather(weighted, len(kinds))))
    back_parts = [group(dot(flat(weighted_all[kind]), w_out, (1, 1))) for kind in kinds]
    backs, weighted_all = gx_sum(*back_parts, y, zl, all_in_ring_order, weighted_all)
    back_pres = [(slope * back).astype(BF16) for slope, back in zip(slopes, backs)]
    back_all = dict(zip(kinds, gx_gather(*back_pres)))

    back_rows = join([flat(back_all[kind]) for kind in kinds], 0)
    acts_all = part(hidden_rows, 1, 0, hidden)
    w_mine, w_theirs = halves(weighted_all, 1)
    t_mine, t_theirs = halves(tokens_all, 1)
    out_got = swap(dot(acts_all, w_theirs, (0, 0)), "c")
    grad_out = (dot(acts_all, w_mine, (0, 0)) + out_got.astype(F32)) * scale
    in_got = swap(dot(t_theirs, back_rows, (0, 0)), "c")
    grad_in = (dot(t_mine, back_rows, (0, 0)) + in_got.astype(F32)) * scale
    return grad_in, grad_out


def solution(mesh):
    fine = Mesh(mesh.devices.reshape(2, 4, 2, 4, 4), ("zl", "y", "c", "x", "zh"))
    gx, gy = ("zl", "y", "c"), ("x", "zh")
    return jax.shard_map(
        per_device,
        mesh=fine,
        in_specs=(P(gy, gx), P(gx, gy), P(gx, gy), P(gy, gx), P(gy, gx), P(None, gx)),
        out_specs=(P(gx, gy), P(gy, gx)),
        check_vma=False,
    )
```

```python
import math

import jax
import jax.numpy as jnp
from jax import lax
from jax.sharding import Mesh
from jax.sharding import PartitionSpec as P

BF16 = jnp.bfloat16
F32 = jnp.float32
RING = 4


def gelu_parts(pre_act):
    cdf = 0.5 * (1.0 + lax.erf(pre_act / math.sqrt(2.0)))
    slopes = cdf + pre_act * jnp.exp(-0.5 * pre_act * pre_act) / math.sqrt(2.0 * math.pi)
    return pre_act * cdf, slopes


def shift(value, axis, by):
    return lax.ppermute(value, axis, [(i, (i + by) % RING) for i in range(RING)])


def swap(value, axis):
    return lax.ppermute(value, axis, [(0, 1), (1, 0)])


def part(value, dim, start, size=1):
    return lax.slice_in_dim(value, start, start + size, axis=dim)


def halves(value, dim):
    size = value.shape[dim] // 2
    return part(value, dim, 0, size), part(value, dim, size, size)


def join(parts, dim):
    return lax.concatenate(parts, dim)


def ring_send(block, axis):
    return [shift(block(k).astype(BF16), axis, k) for k in (1, 3, 2)]


def total(own, got):
    own = own.astype(F32)
    for value in got:
        own = own + value.astype(F32)
    return own


def ring_sum(block, axis):
    return total(block(0), ring_send(block, axis))


def ring_gather(own, axis):
    got = lax.optimization_barrier([shift(own, axis, -k) for k in (1, 3, 2)])
    return [own, got[0], got[2], got[1]]


def pick(value, dim, index, size=1):
    return lax.dynamic_slice_in_dim(value, index, size, axis=dim)


def rolled(value, dim, offset):
    twice = join([value, part(value, dim, 0, RING - 1)], dim)
    return lax.dynamic_slice_in_dim(twice, offset, RING, axis=dim)


def gx_sum(wide, deep, y, zl, work, aside):
    def zl_half(value, dim):
        return lambda m: pick(value, dim, 2 * ((zl + m) % 2), 2)

    wide_block, deep_block = lambda k: pick(wide, 0, (y + k) % RING), zl_half(deep, 0)
    wide_own, deep_own, wide_out, deep_out, aside = lax.optimization_barrier(
        (
            wide_block(0).astype(F32),
            deep_block(0).astype(F32),
            {k: wide_block(k).astype(BF16) for k in range(1, RING)},
            deep_block(1).astype(BF16),
            aside,
        )
    )
    deep_got = swap(deep_out, "zl")
    wide_got, deep_got, done = lax.optimization_barrier(
        (ring_send(lambda k: wide_out[k], "y"), deep_got, work(aside))
    )
    wide = total(wide_own, wide_got)
    deep = total(deep_own, [deep_got])

    wide_block, deep_block = zl_half(wide, 1), lambda k: pick(deep, 1, (y + k) % RING)
    wide_got = swap(wide_block(1).astype(BF16), "zl")
    deep_got, wide_got = lax.optimization_barrier((ring_send(deep_block, "y"), wide_got))
    return (total(wide_block(0), [wide_got]), total(deep_block(0), deep_got)), done


def gx_gather(wide, deep):
    deep_got, wide_got = lax.optimization_barrier((ring_gather(deep, "y"), swap(wide, "zl")))
    wide = join([wide, wide_got], 1)
    deep = join(deep_got, 1)
    wide_got, deep_got = lax.optimization_barrier((ring_gather(wide, "y"), swap(deep, "zl")))
    return join(wide_got, 0), join([deep, deep_got], 0)


def gy_sum(block4s, offsets):
    count = len(block4s)
    first = ring_sum(
        lambda k: join([pick(b, 0, (k - ox) % RING) for b, (ox, _) in zip(block4s, offsets)], 2), "x"
    )
    size = first.shape[2] // count
    columns = [part(first, 2, g * size, size) for g in range(count)]
    return ring_sum(
        lambda k: join([pick(c, 1, (k - oz) % RING) for c, (_, oz) in zip(columns, offsets)], 2), "zh"
    )


def split_groups(blocks, groups):
    size = blocks[0].shape[2] // groups
    return [join([part(b, 2, g * size, size) for b in blocks], 0) for g in range(groups)]


def gy_gather(own, groups):
    return split_groups(ring_gather(join(ring_gather(own, "zh"), 1), "x"), groups)


def ring_order(block4, offset):
    ox, oz = offset
    return rolled(rolled(block4, 0, ox), 1, oz)


def dot(a, b, contract):
    return lax.dot_general(a, b, ((contract[:1], contract[1:]), ((), ())), preferred_element_type=F32)


def per_device(tokens, weight_in, tangent_in, weight_out, tangent_out, curvature):
    core, y, zl = lax.axis_index("c"), lax.axis_index("y"), lax.axis_index("zl")
    gy = lax.axis_index("x") * RING + lax.axis_index("zh")
    rows, width = tokens.shape
    hidden = weight_in.shape[1]
    half = rows // 2
    quarter = half // 2
    scale = 1.0 / math.sqrt(rows * 16)

    keep = lax.dynamic_slice_in_dim(tokens, core * half, half, 0)
    give = lax.dynamic_slice_in_dim(tokens, (1 - core) * half, half, 0)
    curv = lax.dynamic_slice_in_dim(curvature, gy * rows, rows, 0)
    curv_keep = lax.dynamic_slice_in_dim(curv, core * half, half, 0)
    curv_give = lax.dynamic_slice_in_dim(curv, (1 - core) * half, half, 0)

    kinds = ("wide", "deep")
    offsets = {"wide": (y, 2 * zl), "deep": (2 * zl, y)}
    places = [offsets[kind] for kind in kinds]
    got, curv_got = lax.optimization_barrier((swap(give, "c"), swap(curv_give, "c")))
    own_rows = join([keep, got], 1).reshape(1, 1, half, 2 * width)
    curv_own = join([curv_keep, curv_got], 1)
    w_got, t_got = swap(weight_in, "c"), swap(tangent_in, "c")
    column = join(ring_gather(own_rows, "zh"), 1)
    column, w_got, t_got = lax.optimization_barrier((column, w_got, t_got))
    blocks, out_pair = lax.optimization_barrier(
        (ring_gather(column, "x"), join([tangent_out, weight_out], 0))
    )
    toks = dict(zip(kinds, split_groups(blocks, len(kinds))))
    w_in = join([weight_in, w_got], 0)
    t_in = join([tangent_in, t_got], 0)

    def flat(value):
        return value.reshape(-1, value.shape[-1])

    def group(value):
        return value.reshape(RING, RING, quarter, -1)

    def all_in_ring_order(values):
        return join([flat(ring_order(values[kind], offsets[kind])) for kind in kinds], 0)

    pres = [
        group(join([dot(flat(toks[kind]), w_in, (1, 0)), dot(flat(toks[kind]), t_in, (1, 0))], 1))
        for kind in kinds
    ]
    slopes, mixed = [], []
    def beside_first(values):
        return all_in_ring_order(values[0]), swap(values[1], "c")

    pre_sums, (tokens_all, pair_got) = gx_sum(*pres, y, zl, beside_first, (toks, out_pair))
    out_side = join([out_pair, pair_got], 1)
    w_out = part(out_side, 0, hidden, hidden)
    for both in pre_sums:
        pre_act, pre_tan = halves(both, 3)
        acts, slope = gelu_parts(pre_act)
        slopes.append(slope)
        mixed.append(join([acts.astype(BF16), (slope * pre_tan).astype(BF16)], 3))
    hidden_rows = join([flat(value) for value in gx_gather(*mixed)], 0)
    out_parts = [group(value) for value in halves(dot(hidden_rows, out_side, (1, 0)), 0)]
    out_tan = gy_sum(out_parts, places)
    weighted = (curv_own.reshape(out_tan.shape) * out_tan).astype(BF16)
    weighted_all = dict(zip(kinds, gy_gather(weighted, len(kinds))))
    back_parts = [group(dot(flat(weighted_all[kind]), w_out, (1, 1))) for kind in kinds]
    backs, weighted_all = gx_sum(*back_parts, y, zl, all_in_ring_order, weighted_all)
    back_pres = [(slope * back).astype(BF16) for slope, back in zip(slopes, backs)]
    back_all = dict(zip(kinds, gx_gather(*back_pres)))

    back_rows = join([flat(back_all[kind]) for kind in kinds], 0)
    acts_all = part(hidden_rows, 1, 0, hidden)
    w_mine, w_theirs = halves(weighted_all, 1)
    t_mine, t_theirs = halves(tokens_all, 1)
    out_got = swap(dot(acts_all, w_theirs, (0, 0)), "c")
    grad_out = (dot(acts_all, w_mine, (0, 0)) + out_got.astype(F32)) * scale
    in_got = swap(dot(t_theirs, back_rows, (0, 0)), "c")
    grad_in = (dot(t_mine, back_rows, (0, 0)) + in_got.astype(F32)) * scale
    return grad_in, grad_out


def solution(mesh):
    fine = Mesh(mesh.devices.reshape(2, 4, 2, 4, 4), ("zl", "y", "c", "x", "zh"))
    gx, gy = ("zl", "y", "c"), ("x", "zh")
    return jax.shard_map(
        per_device,
        mesh=fine,
        in_specs=(P(gy, gx), P(gx, gy), P(gx, gy), P(gy, gx), P(gy, gx), P(None, gx)),
        out_specs=(P(gx, gy), P(gy, gx)),
        check_vma=False,
    )
```
